32 devices in a mesh: dom: 2 (over y), row: 4 (over x, core), col: 4 (over z).
Axes of the slice: x: 2, y: 2, z: 4, core: 2. Of those that a mesh axis runs over, the one named last changes fastest.
Arguments:
- ext_ext: float32 [4, 2304, 2304], P('dom', 'row', 'col'), parts along dimension 0, may hold values from -0.125 to 0.125
- ext_int: float32 [4, 2304, 768], P('dom', 'row', 'col'), parts along dimension 0, may hold values from -0.21875 to 0.21875
- int_ext: float32 [4, 768, 2304], P('dom', 'row', 'col'), parts along dimension 0, may hold values from -0.125 to 0.125
- int_int: float32 [4, 768, 768], P('dom', 'row', 'col'), parts along dimension 0, may hold values from -2 to 2, as said below
- boundary_data: float32 [4, 2304, 128], P('dom', 'row', 'col'), parts along dimension 0, may hold values from -6 to 6
- leaf_ext_ext: float32 [32, 2, 576, 576], P(('dom', 'row', 'col')), parts along dimension 0, may hold values from -0.25 to 0.25
- leaf_ext_int: float32 [32, 2, 576, 192], P(('dom', 'row', 'col')), parts along dimension 0, may hold values from -0.4375 to 0.4375
- leaf_int_ext: float32 [32, 2, 192, 576], P(('dom', 'row', 'col')), parts along dimension 0, may hold values from -0.25 to 0.25
- leaf_int_int: float32 [32, 2, 192, 192], P(('dom', 'row', 'col')), parts along dimension 0, may hold values from -2 to 2, as said below
Outputs:
- parent_map: float32 [4, 2, 2304, 2304], P('dom', None, 'row', 'col'), parts along dimension 0
- solve_op: float32 [4, 768, 2304], P('dom', 'row', 'col'), parts along dimension 0
- interface_values: float32 [1536, 128], P(('dom', 'row'), 'col'), parts along dimension 0
- leaf_parent: float32 [32, 2, 2, 576, 576], P(('dom', 'row', 'col')), parts along dimension 0
- leaf_solve: float32 [32, 2, 192, 576], P(('dom', 'row', 'col')), parts along dimension 0
The draws below stay inside these ranges and needn't reach their ends.
There are 2 independent parts, one for each index of `dom`. The reference program is written for one: setup_inputs(seed, part) draws one part's arguments, and reference() takes and returns one part's arrays. A program takes and returns all parts, laid end to end along the dimension named above; each array names one. Nothing has to cross between parts.
Inputs may be any that keep to these rules, and one draw needn't show every extreme that they name: `int_int`: off-diagonal entries are small against a diagonal between 1 and 2 in each child's map. `leaf_int_int`: off-diagonal entries are small against a diagonal between 1 and 2 in each child's map.
All inputs are finite; a program needn't handle non-finite values.
Results may differ from the reference program's by a relative error of at most 0.00022.
Values sent between devices are 32-bit elements; how exact they have to be, the bound alone decides.
A program may use at most 128 MiB of HBM per device.

```python
import jax
import jax.numpy as jnp
from jax import lax

SIDE = 768
LEAF = 192
SOURCES = 128
ITERS = 2
BOXES = 16


def dominant(key, lead, size):
    first, second = jax.random.split(key)
    spread = 0.4 / size ** 0.5
    off_diag = jax.random.normal(first, lead + (size, size), jnp.float32) * spread
    diag_vals = jax.random.uniform(second, lead + (size,), jnp.float32, 1.0, 2.0)
    eye = jnp.eye(size, dtype=jnp.float32)
    return off_diag * (1.0 - eye) + diag_vals[..., :, None] * eye


def draw_int_int(key, part):
    return dominant(jax.random.fold_in(key, 17), (2,), SIDE)


def draw_leaf_int_int(key, part):
    return dominant(jax.random.fold_in(key, 29), (BOXES, 2), LEAF)


def block_levels(rng, extent, cuts, least, high):
    gain, own = 1.0, jax.random.fold_in(rng, 6)
    for axis_at, parts in cuts:
        draws = jnp.exp(jax.random.uniform(jax.random.fold_in(own, axis_at), (parts,), jnp.float32, least / len(cuts), high / len(cuts)))
        gain = gain * jnp.repeat(draws, extent[axis_at] // parts).reshape([-1 if axis == axis_at else 1 for axis in range(len(extent))])
    return gain


def scatter_about(key, extent, scale, limit, cuts=(), kind=jnp.bfloat16):
    level = block_levels(key, extent, cuts, -0.22, 0.18) if cuts else 1.0
    result = jax.random.normal(key, extent, jnp.float32) * scale * level
    return jnp.minimum(jnp.maximum(result, -limit), limit).astype(kind)


def setup_inputs(seed: int = 0, part: int = 0) -> dict:
    streams_of = jax.random.split(jax.random.key(seed), 10)
    part_keys = jax.random.split(jax.random.fold_in(streams_of[9], part), 10)
    ext_ext = scatter_about(part_keys[0], (2, 3 * SIDE, 3 * SIDE), (3 * SIDE) ** -0.5, 0.125, ((1, 4), (2, 4)), jnp.float32)
    ext_int = scatter_about(part_keys[1], (2, 3 * SIDE, SIDE), SIDE ** -0.5, 0.21875, ((1, 4), (2, 4)), jnp.float32)
    int_ext = scatter_about(part_keys[2], (2, SIDE, 3 * SIDE), (3 * SIDE) ** -0.5, 0.125, ((1, 4), (2, 4)), jnp.float32)
    int_int = draw_int_int(jax.random.fold_in(jax.random.fold_in(streams_of[9], part), 71), part)
    boundary_data = scatter_about(part_keys[4], (2, 3 * SIDE, SOURCES), 1.0, 6.0, ((1, 4), (2, 4)), jnp.float32)
    leaf_ext_ext = scatter_about(part_keys[5], (BOXES, 2, 3 * LEAF, 3 * LEAF), (3 * LEAF) ** -0.5, 0.25, ((0, 16),), jnp.float32)
    leaf_ext_int = scatter_about(part_keys[6], (BOXES, 2, 3 * LEAF, LEAF), LEAF ** -0.5, 0.4375, ((0, 16),), jnp.float32)
    leaf_int_ext = scatter_about(part_keys[7], (BOXES, 2, LEAF, 3 * LEAF), (3 * LEAF) ** -0.5, 0.25, ((0, 16),), jnp.float32)
    leaf_int_int = draw_leaf_int_int(jax.random.fold_in(jax.random.fold_in(streams_of[9], part), 71), part)
    return dict(ext_ext=ext_ext, ext_int=ext_int, int_ext=int_ext, int_int=int_int, boundary_data=boundary_data, leaf_ext_ext=leaf_ext_ext, leaf_ext_int=leaf_ext_int, leaf_int_ext=leaf_int_ext, leaf_int_int=leaf_int_int)


def matmul(a, b):
    return jnp.dot(a, b, precision=lax.Precision.HIGHEST, preferred_element_type=jnp.float32)


def newton(joint):
    size = joint.shape[0]
    eye = jnp.eye(size, dtype=jnp.float32)
    current = eye / jnp.diagonal(joint)[None, :]
    for step in range(ITERS):
        product = matmul(joint, current)
        current = 2.0 * current - matmul(current, product)
    return current


def merge_local(ee, ei, ie, ii):
    side = ii.shape[1]
    third = ee.shape[1]
    inverse = newton(ii[0] + ii[1])
    coupling = jnp.concatenate([ie[0], ie[1]], axis=1)
    solution = -matmul(inverse, coupling)
    solve = jnp.stack([solution[:, :third], solution[:, third:]])
    lifted = matmul(ei.reshape(2 * third, side), solution)
    lifted = lifted.reshape(2, third, 2, third).transpose(0, 2, 1, 3)
    pairs = jnp.eye(2, dtype=jnp.float32)
    parent = lifted + pairs[:, :, None, None] * ee[:, None]
    return parent, solve, solution


def leaf_merge(group):
    parent, solve, solution = merge_local(group[0], group[1], group[2], group[3])
    return parent, solve


def reference(ext_ext, ext_int, int_ext, int_int, boundary_data, leaf_ext_ext, leaf_ext_int, leaf_int_ext, leaf_int_int):
    parent_map, solve_op, solution = merge_local(ext_ext, ext_int, int_ext, int_int)
    interface_values = matmul(solution, boundary_data.reshape(6 * SIDE, SOURCES))
    leaf_parent, leaf_solve = lax.map(leaf_merge, (leaf_ext_ext, leaf_ext_int, leaf_int_ext, leaf_int_int))
    return parent_map, solve_op, interface_values, leaf_parent, leaf_solve
```

```python
import functools

import jax
import jax.numpy as jnp
from jax import lax
from jax.experimental import pallas as pl
from jax.experimental.pallas import tpu as pltpu
from jax.sharding import PartitionSpec as P

MESH = pl.DeviceIdType.MESH
BF = jnp.bfloat16
F32 = jnp.float32
ITERS = 2


def split(x):
    hi = x.astype(BF)
    return hi, (x - hi.astype(F32)).astype(BF)


def dot(a, b):
    return jnp.dot(a, b, preferred_element_type=F32)


def dot3(ah, al, bh, bl):
    return dot(ah, bh) + (dot(ah, bl) + dot(al, bh))


def first_step(joint):
    n = joint.shape[0]
    eye = lax.broadcasted_iota(jnp.int32, (n, n), 0) == lax.broadcasted_iota(jnp.int32, (n, n), 1)
    kept = jnp.where(eye, joint, 0.0)
    down = 1.0 / jnp.sum(kept, axis=1, keepdims=True)
    across = 1.0 / jnp.sum(kept, axis=0, keepdims=True)
    return jnp.where(eye, 2.0 * across, 0.0) - down * joint * across


def up128(n):
    return -(-n // 128) * 128


def kernel(
    R, C, M, PK,
    ee, ei, ie, ii, bd, lee, lei, lie, lii,
    parent, solve, iv, lparent, lsolve,
    eg, cg, jg, bdp, bdr, ivs, ivr,
    ein, cin, jin, bdin, eev, leev, leiv, liev, liiv,
    pv, sv, ivv, lpv, lsv,
    big, jh, jl, xh, xl, wh, wl, ch, cl, sh, sl,
    lch, lcl, lsh, lsl, ah, al,
    load, e_recv, e_up, e_dn, jz_send, jz_recv, jp_send, jp_recv, cp_send, cp_recv,
    b_sem, iv_send, iv_recv, out_sem, lp_sem, pm_sem,
):
    d, r, z = lax.axis_index("dom"), lax.axis_index("row"), lax.axis_index("col")
    mate = r + 1 - 2 * lax.rem(r, 2)
    core = lax.rem(r, 2)
    chip = lax.div(r, 2)
    X = R // 2
    h, w = ii.shape[1], ii.shape[2]
    t, u = ei.shape[1], ei.shape[2]
    T = up128(t)
    n = R * h
    tm = t // M
    src_cols = bd.shape[2]

    loads = [
        pltpu.make_async_copy(s, v, load.at[k])
        for k, (s, v) in enumerate(
            [(ii, jin), (ei, ein), (ie, cin), (bd, bdin), (lii, liiv), (lie, liev), (lei, leiv), (lee, leev), (ee, eev)]
        )
    ]
    for c in loads:
        c.start()

    barrier = pltpu.get_barrier_semaphore()

    @pl.loop(0, R)
    def _(a):
        @pl.loop(0, C)
        def _(b):
            @pl.when(jnp.logical_or(a != r, b != z))
            def _():
                pl.semaphore_signal(barrier, inc=1, device_id={"row": a, "col": b}, device_id_type=MESH)

    loads[0].wait()
    half = h // 2
    own_j = jin[0] + jin[1]
    jg[r, z, :, :w] = own_j[:half]
    jg[r, z, :, w:] = own_j[half:]
    loads[1].wait()
    eg[z, :, :u] = ein[0]
    eg[z, :, u:] = ein[1]
    loads[2].wait()
    here = pl.multiple_of(r * h, h)
    cg[pl.ds(here, h), :t] = cin[0]
    cg[pl.ds(here, h), t:] = cin[1]
    loads[3].wait()
    part = t // (PK // 2)
    for q in range(PK):
        a, o = q // (PK // 2), (q % (PK // 2)) * part
        bdp[:, q * src_cols:(q + 1) * src_cols] = bdin[a, o:o + part]

    pl.semaphore_wait(barrier, R * C - 1)

    def jz(to):
        return pltpu.make_async_remote_copy(
            jg.at[r, z], jg.at[r, z], jz_send.at[to], jz_recv.at[z], device_id={"col": to}, device_id_type=MESH)

    def jz_in(frm):
        return pltpu.make_async_remote_copy(
            jg.at[r, frm], jg.at[r, frm], jz_send.at[frm], jz_recv.at[frm], device_id={"col": frm}, device_id_type=MESH)

    @pl.loop(0, C)
    def _(b):
        @pl.when(b != z)
        def _():
            jz(b).start()

    def e_copy(src, m, up):
        rows = pl.ds(pl.multiple_of(m * tm, 8), tm)
        to = z + 1 if up else z - 1
        return pltpu.make_async_remote_copy(
            eg.at[src, rows], eg.at[src, rows], (e_up if up else e_dn).at[src, m], e_recv.at[src, m],
            device_id={"col": to}, device_id_type=MESH)

    can_up, can_dn = z < C - 1, z > 0

    @pl.loop(0, M)
    def _(m):
        @pl.when(can_up)
        def _():
            e_copy(z, m, True).start()

        @pl.when(can_dn)
        def _():
            e_copy(z, m, False).start()

    def forward(s, lo, hi):
        @pl.loop(lo, hi)
        def _(m):
            @pl.when(jnp.logical_and(can_up, z >= s))
            def _():
                e_copy(z - s, m, True).wait_recv()
                e_copy(z - s, m, True).start()

            @pl.when(jnp.logical_and(can_dn, z + s <= C - 1))
            def _():
                e_copy(z + s, m, False).wait_recv()
                e_copy(z + s, m, False).start()

    def c_copy(row, to, k):
        rows = pl.ds(pl.multiple_of(row * h, h), h)
        return pltpu.make_async_remote_copy(
            cg.at[rows], cg.at[rows], cp_send.at[k], cp_recv.at[row], device_id={"row": to}, device_id_type=MESH)

    def j_copy(row, to, k):
        return pltpu.make_async_remote_copy(
            jg.at[row], jg.at[row], jp_send.at[k], jp_recv.at[row], device_id={"row": to}, device_id_type=MESH)

    def spread_own(copy):
        @pl.loop(0, X)
        def _(x):
            @pl.when(x != chip)
            def _():
                copy(r, 2 * x + core, x).start()

        copy(r, mate, chip).start()

    def relay(copy):
        @pl.loop(0, X)
        def _(x):
            @pl.when(x != chip)
            def _():
                copy(2 * x + core, mate, X + x).wait_recv()
                copy(2 * x + core, mate, X + x).start()

    def settle(copy):
        copy(mate, mate, chip).wait_recv()

        @pl.loop(0, X)
        def _(x):
            @pl.when(x != chip)
            def _():
                copy(2 * x + 1 - core, mate, X + x).wait_recv()

    def finish(copy):
        copy(r, mate, chip).wait_send()

        @pl.loop(0, X)
        def _(x):
            @pl.when(x != chip)
            def _():
                copy(r, 2 * x + core, x).wait_send()
                copy(2 * x + core, mate, X + x).wait_send()

    spread_own(c_copy)

    crossed = pltpu.make_async_remote_copy(
        bdp, bdr, b_sem.at[0], b_sem.at[1], device_id={"row": z, "col": r}, device_id_type=MESH)

    @pl.when(r != z)
    def _():
        crossed.start()

    @pl.when(r == z)
    def _():
        bdr[...] = bdp[...]

    loads[4].wait()
    loads[5].wait()
    lj = liiv[0] + liiv[1]
    x1 = first_step(lj)
    x1h, x1l = split(x1)
    ljh, ljl = split(lj)
    lw = dot3(ljh, ljl, x1h, x1l)
    x2 = dot3(x1h, x1l, *split(lw)) - 2.0 * x1
    x2h, x2l = split(x2)
    nl = lj.shape[0]
    tl = lie.shape[2]
    TL = up128(tl)
    for b in range(2):
        lch[:, b * TL:b * TL + tl], lcl[:, b * TL:b * TL + tl] = split(liev[b])
        got = dot3(x2h, x2l, lch[:, b * TL:b * TL + tl], lcl[:, b * TL:b * TL + tl])
        lsv[b] = got
        lsh[:, b * TL:b * TL + tl], lsl[:, b * TL:b * TL + tl] = split(got)
    ls_out = pltpu.make_async_copy(lsv, lsolve, out_sem.at[0])
    ls_out.start()

    @pl.loop(0, C)
    def _(b):
        @pl.when(b != z)
        def _():
            jz_in(b).wait_recv()

    spread_own(j_copy)

    loads[6].wait()
    loads[7].wait()
    for a in range(2):
        @pl.loop(0, tl // nl)
        def _(m):
            rows = pl.ds(pl.multiple_of(m * nl, nl), nl)
            eh, el = split(leiv[a, rows])
            for b in range(2):
                cols = slice(b * TL, b * TL + tl)
                got = dot3(eh, el, lsh[:, cols], lsl[:, cols])
                lpv[a, b, rows] = got + leev[a, rows] if a == b else got
                pltpu.make_async_copy(lpv.at[a, b, rows], lparent.at[a, b, rows], lp_sem.at[2 * a + b, m]).start()

    mh = M // 2
    forward(1, 0, mh)
    relay(c_copy)
    settle(c_copy)
    for b in range(2):
        @pl.loop(0, R)
        def _(k):
            rows = pl.ds(pl.multiple_of(k * h, h), h)
            ch[rows, b * T:b * T + t], cl[rows, b * T:b * T + t] = split(cg[rows, b * t:(b + 1) * t])
    forward(1, mh, M)
    relay(j_copy)
    settle(j_copy)
    for a in range(R):
        for b in range(C):
            big[a * h:a * h + half, b * w:(b + 1) * w] = jg[a, b, :, :w]
            big[a * h + half:(a + 1) * h, b * w:(b + 1) * w] = jg[a, b, :, w:]
    joint = big[...]
    jh[...], jl[...] = split(joint)
    x1 = first_step(joint)
    big[...] = x1
    xh[...], xl[...] = split(x1)

    @pl.loop(0, R)
    def _(k):
        rows = pl.ds(pl.multiple_of(k * h, h), h)
        wh[rows], wl[rows] = split(dot3(jh[rows], jl[rows], xh[...], xl[...]))

    for s in range(2, C - 1):
        forward(s, 0, mh)

    @pl.loop(0, R)
    def _(k):
        rows = pl.ds(pl.multiple_of(k * h, h), h)
        jh[rows], jl[rows] = split(dot3(xh[rows], xl[rows], wh[...], wl[...]) - 2.0 * big[rows])

    for s in range(2, C - 1):
        forward(s, mh, M)

    @pl.loop(0, R)
    def _(k):
        rows = pl.ds(pl.multiple_of(k * h, h), h)
        for b in range(2):
            cols = slice(b * T, b * T + t)
            got = dot3(jh[rows], jl[rows], ch[:, cols], cl[:, cols])
            sh[rows, cols], sl[rows, cols] = split(got)

            @pl.when(k == r)
            def _():
                sv[b] = got

    s_out = pltpu.make_async_copy(sv, solve, out_sem.at[1])
    s_out.start()

    @pl.when(r != z)
    def _():
        crossed.wait_recv()

    flat = jnp.concatenate([bdr[:, q * src_cols:(q + 1) * src_cols] for q in range(PK)], axis=0)
    fh, fl = split(flat)
    quarter = h // PK
    for k in range(R):
        rows = slice(k * h, (k + 1) * h)
        got = dot3(sh[rows, :t], sl[rows, :t], fh[:t], fl[:t])
        got += dot3(sh[rows, T:T + t], sl[rows, T:T + t], fh[t:], fl[t:])
        for q in range(PK):
            ivs[k, :, q * src_cols:(q + 1) * src_cols] = got[q * quarter:(q + 1) * quarter]

    def iv_copy(k):
        return pltpu.make_async_remote_copy(
            ivs.at[k], ivr.at[z], iv_send.at[k], iv_recv.at[z], device_id={"row": k, "col": r}, device_id_type=MESH)

    def iv_in(c):
        return pltpu.make_async_remote_copy(
            ivs.at[r], ivr.at[c], iv_send.at[c], iv_recv.at[c], device_id={"row": z, "col": c}, device_id_type=MESH)

    for k in range(R):
        own = jnp.logical_and(r == k, r == z)

        @pl.when(jnp.logical_not(own))
        def _():
            iv_copy(k).start()

        @pl.when(own)
        def _():
            ivr[z] = ivs[k]

    loads[8].wait()

    @pl.loop(0, M)
    def _(m):
        @pl.when(z == C - 1)
        def _():
            @pl.loop(0, C - 1)
            def _(i):
                s = C - 2 - i
                e_copy(s, m, False).wait_recv()

        @pl.when(z == 0)
        def _():
            @pl.loop(1, C)
            def _(s):
                e_copy(s, m, True).wait_recv()

        rows = pl.ds(pl.multiple_of(m * tm, 8), tm)
        for c in range(C):
            for a in range(2):
                o = slice(a * tm, (a + 1) * tm)
                ah[o, c * u:(c + 1) * u], al[o, c * u:(c + 1) * u] = split(eg[c, rows, a * u:(a + 1) * u])
        for b in range(2):
            cols = slice(b * T, b * T + t)
            got = dot3(ah[...], al[...], sh[:, cols], sl[:, cols])
            for a in range(2):
                one = got[a * tm:(a + 1) * tm]
                pv[a, b, rows] = one + eev[a, rows] if a == b else one
                pltpu.make_async_copy(pv.at[a, b, rows], parent.at[a, b, rows], pm_sem.at[2 * a + b, m]).start()

    @pl.loop(0, C)
    def _(c):
        @pl.when(jnp.logical_not(jnp.logical_and(r == z, c == z)))
        def _():
            iv_in(c).wait_recv()

    total = ivr[0]
    for c in range(1, C):
        total = total + ivr[c]
    for q in range(PK):
        ivv[q * quarter:(q + 1) * quarter] = total[:, q * src_cols:(q + 1) * src_cols]
    iv_out = pltpu.make_async_copy(ivv, iv, out_sem.at[2])
    iv_out.start()

    @pl.loop(0, C)
    def _(b):
        @pl.when(b != z)
        def _():
            jz(b).wait_send()

    finish(c_copy)
    finish(j_copy)

    @pl.when(r != z)
    def _():
        crossed.wait_send()

    for k in range(R):
        @pl.when(jnp.logical_not(jnp.logical_and(r == k, r == z)))
        def _():
            iv_copy(k).wait_send()

    @pl.loop(0, M)
    def _(m):
        @pl.when(can_up)
        def _():
            @pl.loop(0, z + 1)
            def _(s):
                e_copy(s, m, True).wait_send()

        @pl.when(can_dn)
        def _():
            @pl.loop(z, C)
            def _(s):
                e_copy(s, m, False).wait_send()

        rows = pl.ds(pl.multiple_of(m * tm, 8), tm)
        for a in range(2):
            for b in range(2):
                pltpu.make_async_copy(pv.at[a, b, rows], parent.at[a, b, rows], pm_sem.at[2 * a + b, m]).wait()

    @pl.loop(0, tl // nl)
    def _(m):
        rows = pl.ds(pl.multiple_of(m * nl, nl), nl)
        for a in range(2):
            for b in range(2):
                pltpu.make_async_copy(lpv.at[a, b, rows], lparent.at[a, b, rows], lp_sem.at[2 * a + b, m]).wait()

    ls_out.wait()
    s_out.wait()
    iv_out.wait()


def fused(R, C, ee, ei, ie, ii, bd, lee, lei, lie, lii):
    lee, lei, lie, lii = lee[0], lei[0], lie[0], lii[0]
    h, w = ii.shape[1:]
    t, u = ei.shape[1:]
    nl, tl = lie.shape[1:]
    T, TL = up128(t), up128(tl)
    n = R * h
    q = bd.shape[2]
    PK = 128 // q
    M = 6
    tm = t // M
    V = pltpu.VMEM
    D = pltpu.SemaphoreType.DMA
    scratch = [
        V((C, t, 2 * u), F32), V((n, 2 * t), F32), V((R, C, h // 2, 2 * w), F32),
        V((2 * t // PK, 128), F32), V((2 * t // PK, 128), F32), V((R, h // PK, 128), F32), V((C, h // PK, 128), F32),
        V(ei.shape, F32), V(ie.shape, F32), V(ii.shape, F32), V(bd.shape, F32), V(ee.shape, F32),
        V(lee.shape, F32), V(lei.shape, F32), V(lie.shape, F32), V(lii.shape, F32),
        V((2, 2, t, t), F32), V((2, h, t), F32), V((h, q), F32), V((2, 2, tl, tl), F32), V((2, nl, tl), F32),
        V((n, n), F32), V((n, n), BF), V((n, n), BF), V((n, n), BF), V((n, n), BF), V((n, n), BF), V((n, n), BF),
        V((n, 2 * T), BF), V((n, 2 * T), BF), V((n, 2 * T), BF), V((n, 2 * T), BF),
        V((nl, 2 * TL), BF), V((nl, 2 * TL), BF), V((nl, 2 * TL), BF), V((nl, 2 * TL), BF),
        V((2 * tm, n), BF), V((2 * tm, n), BF),
        D((9,)), D((C, M)), D((C, M)), D((C, M)), D((C,)), D((C,)), D((R,)), D((R,)), D((R,)), D((R,)),
        D((2,)), D((R,)), D((C,)), D((3,)), D((4, tl // nl)), D((4, M)),
    ]
    outs = (
        jax.ShapeDtypeStruct((2, 2, t, t), F32),
        jax.ShapeDtypeStruct((2, h, t), F32),
        jax.ShapeDtypeStruct((h, q), F32),
        jax.ShapeDtypeStruct((2, 2, tl, tl), F32),
        jax.ShapeDtypeStruct((2, nl, tl), F32),
    )
    got = pl.pallas_call(
        functools.partial(kernel, R, C, M, PK),
        out_shape=outs,
        in_specs=[pl.BlockSpec(memory_space=pl.ANY)] * 9,
        out_specs=[pl.BlockSpec(memory_space=pl.ANY)] * 5,
        scratch_shapes=scratch,
        compiler_params=pltpu.CompilerParams(
            collective_id=0, has_side_effects=True, vmem_limit_bytes=60 * 1024 * 1024),
        cost_estimate=pl.CostEstimate(flops=18 * n * n * t * 4, bytes_accessed=24 * t * t * 4, transcendentals=0),
    )(ee, ei, ie, ii, bd, lee, lei, lie, lii)
    return got[0], got[1], got[2], got[3][None], got[4][None]


def fits(R, C, shapes):
    h, w = shapes[3][1] // R, shapes[3][2] // C
    t, u = shapes[1][1] // R, shapes[1][2] // C
    q = shapes[4][2] // C
    nl, tl = shapes[7][2:]
    boxes = shapes[5][0]
    return (
        R == C and R % 2 == 0 and C >= 3 and h == w == u and h % 16 == 0 and (2 * u) % 128 == 0 and t % 48 == 0
        and 128 % q == 0 and h % (8 * (128 // q)) == 0 and (2 * t) % (8 * (128 // q)) == 0
        and (128 // q) % 2 == 0 and tl % nl == 0 and nl % 16 == 0
    )


def matmul(a, b):
    return jnp.dot(a, b, precision=lax.Precision.HIGHEST, preferred_element_type=jnp.float32)


def panel(block):
    return lax.all_gather(block, "col", axis=1, tiled=True)


def fold_product(left_rows, right_block):
    return matmul(left_rows, lax.all_gather(right_block, "row", axis=0, tiled=True))


def product(left_block, right_block):
    return fold_product(panel(left_block), right_block)


def merge_local(ee, ei, ie, ii):
    side = ii.shape[1]
    third = ee.shape[1]
    joint = ii[0] + ii[1]
    eye = jnp.eye(side, dtype=jnp.float32)
    current = eye / jnp.diagonal(joint)[None, :]
    for step in range(ITERS):
        current = 2.0 * current - matmul(current, matmul(joint, current))
    coupling = jnp.concatenate([ie[0], ie[1]], axis=1)
    solution = -matmul(current, coupling)
    solve = jnp.stack([solution[:, :third], solution[:, third:]])
    lifted = matmul(ei.reshape(2 * third, side), solution)
    lifted = lifted.reshape(2, third, 2, third).transpose(0, 2, 1, 3)
    pairs = jnp.eye(2, dtype=jnp.float32)
    parent = lifted + pairs[:, :, None, None] * ee[:, None]
    return (parent, solve)


def shards(
    ext_ext,
    ext_int,
    int_ext,
    int_int,
    boundary_data,
    leaf_ext_ext,
    leaf_ext_int,
    leaf_int_ext,
    leaf_int_int,
):
    n_col = lax.axis_size("col")
    joint = int_int[0] + int_int[1]
    rows_here = joint.shape[0]
    cols_here = joint.shape[1]
    third = ext_ext.shape[2]
    coupling = jnp.concatenate([int_ext[0], int_ext[1]], axis=1)
    global_row = lax.axis_index("row") * rows_here + lax.broadcasted_iota(jnp.int32, joint.shape, 0)
    global_col = lax.axis_index("col") * cols_here + lax.broadcasted_iota(jnp.int32, joint.shape, 1)
    on_diag = global_row == global_col
    current = jnp.where(on_diag, 1.0 / jnp.where(on_diag, joint, 1.0), 0.0)
    for step in range(ITERS):
        current = 2.0 * current - product(current, product(joint, current))
    solution = -product(current, coupling)
    leaf_parent, leaf_solve = jax.vmap(merge_local)(
        leaf_ext_ext, leaf_ext_int, leaf_int_ext, leaf_int_int
    )
    solve_op = jnp.stack([solution[:, :third], solution[:, third:]])
    ext_rows = ext_int.shape[1]
    lifted = product(ext_int.reshape(2 * ext_rows, ext_int.shape[2]), solution)
    lifted = lifted.reshape(2, ext_rows, 2, third).transpose(0, 2, 1, 3)
    pairs = jnp.eye(2, dtype=jnp.float32)
    parent_map = lifted + pairs[:, :, None, None] * ext_ext[:, None]
    operator_rows = panel(solution)
    operator_rows = operator_rows.reshape(rows_here, n_col, 2, third).transpose(0, 2, 1, 3)
    operator_rows = operator_rows.reshape(rows_here, 2, n_col * third)
    interface_values = jnp.einsum(
        "pcn,cnq->pq",
        operator_rows,
        lax.all_gather(boundary_data, "row", axis=1, tiled=True),
        precision=lax.Precision.HIGHEST,
    )
    return (parent_map, solve_op, interface_values, leaf_parent, leaf_solve)


def solution(mesh):
    in_specs = (
        P("dom", "row", "col"),
        P("dom", "row", "col"),
        P("dom", "row", "col"),
        P("dom", "row", "col"),
        P("dom", "row", "col"),
        P(("dom", "row", "col"), None, None, None),
        P(("dom", "row", "col"), None, None, None),
        P(("dom", "row", "col"), None, None, None),
        P(("dom", "row", "col"), None, None, None),
    )
    out_specs = (
        P("dom", None, "row", "col"),
        P("dom", "row", "col"),
        P(("dom", "row"), "col"),
        P(("dom", "row", "col"), None, None, None, None),
        P(("dom", "row", "col"), None, None, None),
    )

    def run(*args):
        shapes = [a.shape for a in args]
        R, C = mesh.shape["row"], mesh.shape["col"]
        one_box = shapes[5][0] == mesh.shape["dom"] * R * C
        two_maps = shapes[0][0] == 2 * mesh.shape["dom"]
        body = functools.partial(fused, R, C) if one_box and two_maps and fits(R, C, shapes) else shards
        return jax.shard_map(body, mesh=mesh, in_specs=in_specs, out_specs=out_specs, check_vma=False)(*args)

    return run
```

```python
import functools

import jax
import jax.numpy as jnp
from jax import lax
from jax.experimental import pallas as pl
from jax.experimental.pallas import tpu as pltpu
from jax.sharding import PartitionSpec as P

MESH = pl.DeviceIdType.MESH
BF = jnp.bfloat16
F32 = jnp.float32
ITERS = 2


def split(x):
    hi = x.astype(BF)
    return hi, (x - hi.astype(F32)).astype(BF)


def dot(a, b):
    return jnp.dot(a, b, preferred_element_type=F32)


def dot3(ah, al, bh, bl):
    return dot(ah, bh) + (dot(ah, bl) + dot(al, bh))


def dot_t(a, b):
    return lax.dot_general(a, b, (((1,), (1,)), ((), ())), preferred_element_type=F32)


def dot3t(ah, al, bh, bl):
    return dot_t(ah, bh) + (dot_t(ah, bl) + dot_t(al, bh))


def first_step(joint):
    n = joint.shape[0]
    eye = lax.broadcasted_iota(jnp.int32, (n, n), 0) == lax.broadcasted_iota(jnp.int32, (n, n), 1)
    kept = jnp.where(eye, joint, 0.0)
    down = 1.0 / jnp.sum(kept, axis=1, keepdims=True)
    across = 1.0 / jnp.sum(kept, axis=0, keepdims=True)
    return jnp.where(eye, 2.0 * across, 0.0) - down * joint * across


def up128(n):
    return -(-n // 128) * 128


def kernel(
    R, C, M,
    ee, ei, ie, ii, bd, lee, lei, lie, lii,
    parent, solve, iv, lparent, lsolve,
    eg, cg, jg, bdp, bdr, ivs, ivr,
    ein, cin, jin, eev, leev, leiv, let, liev, liiv,
    pv, sv, ivv, lpv, lsv,
    big, jh, jl, xh, xl, wh, wl, ch, cl, sh, sl,
    lch, lcl, lsh, lsl, ah, al,
    load, e_recv, e_up, e_dn, jz_send, jz_recv, jp_send, jp_recv, cp_send, cp_recv,
    b_sem, iv_send, iv_recv, out_sem, lp_sem, pm_sem,
):
    d, r, z = lax.axis_index("dom"), lax.axis_index("row"), lax.axis_index("col")
    mate = r + 1 - 2 * lax.rem(r, 2)
    core = lax.rem(r, 2)
    chip = lax.div(r, 2)
    X = R // 2
    h, w = ii.shape[1], ii.shape[2]
    t, u = ei.shape[2], ei.shape[1]
    T = up128(t)
    n = R * h
    tm = t // M

    loads = [
        pltpu.make_async_copy(s, v, load.at[k])
        for k, (s, v) in enumerate(
            [(ii, jin), (ei, ein), (ie, cin), (bd, bdp), (lii, liiv), (lie, liev), (lei, leiv), (lee, leev), (ee, eev)]
        )
    ]
    for c in loads:
        c.start()

    barrier = pltpu.get_barrier_semaphore()

    @pl.loop(0, R)
    def _(a):
        @pl.loop(0, C)
        def _(b):
            @pl.when(jnp.logical_or(a != r, b != z))
            def _():
                pl.semaphore_signal(barrier, inc=1, device_id={"row": a, "col": b}, device_id_type=MESH)

    loads[0].wait()
    half = h // 2
    own_j = jin[0] + jin[1]
    jg[r, z, :, :w] = own_j[:half]
    jg[r, z, :, w:] = own_j[half:]
    loads[1].wait()
    eg[z, :, :u] = ein[0].T
    eg[z, :, u:] = ein[1].T
    loads[2].wait()
    here = pl.multiple_of(r * h, h)
    cg[pl.ds(here, h), :t] = cin[0]
    cg[pl.ds(here, h), t:] = cin[1]
    loads[3].wait()

    pl.semaphore_wait(barrier, R * C - 1)

    def jz(to):
        return pltpu.make_async_remote_copy(
            jg.at[r, z], jg.at[r, z], jz_send.at[to], jz_recv.at[z], device_id={"col": to}, device_id_type=MESH)

    def jz_in(frm):
        return pltpu.make_async_remote_copy(
            jg.at[r, frm], jg.at[r, frm], jz_send.at[frm], jz_recv.at[frm], device_id={"col": frm}, device_id_type=MESH)

    @pl.loop(0, C)
    def _(b):
        @pl.when(b != z)
        def _():
            jz(b).start()

    def e_copy(src, m, up):
        rows = pl.ds(pl.multiple_of(m * tm, 8), tm)
        to = z + 1 if up else z - 1
        return pltpu.make_async_remote_copy(
            eg.at[src, rows], eg.at[src, rows], (e_up if up else e_dn).at[src, m], e_recv.at[src, m],
            device_id={"col": to}, device_id_type=MESH)

    can_up, can_dn = z < C - 1, z > 0

    @pl.loop(0, M)
    def _(m):
        @pl.when(can_up)
        def _():
            e_copy(z, m, True).start()

        @pl.when(can_dn)
        def _():
            e_copy(z, m, False).start()

    def forward(s, lo, hi):
        @pl.loop(lo, hi)
        def _(m):
            @pl.when(jnp.logical_and(can_up, z >= s))
            def _():
                e_copy(z - s, m, True).wait_recv()
                e_copy(z - s, m, True).start()

            @pl.when(jnp.logical_and(can_dn, z + s <= C - 1))
            def _():
                e_copy(z + s, m, False).wait_recv()
                e_copy(z + s, m, False).start()

    def c_copy(row, to, k):
        rows = pl.ds(pl.multiple_of(row * h, h), h)
        return pltpu.make_async_remote_copy(
            cg.at[rows], cg.at[rows], cp_send.at[k], cp_recv.at[row], device_id={"row": to}, device_id_type=MESH)

    def j_copy(row, to, k):
        return pltpu.make_async_remote_copy(
            jg.at[row], jg.at[row], jp_send.at[k], jp_recv.at[row], device_id={"row": to}, device_id_type=MESH)

    def spread_own(copy):
        @pl.loop(0, X)
        def _(x):
            @pl.when(x != chip)
            def _():
                copy(r, 2 * x + core, x).start()

        copy(r, mate, chip).start()

    def relay(copy):
        @pl.loop(0, X)
        def _(x):
            @pl.when(x != chip)
            def _():
                copy(2 * x + core, mate, X + x).wait_recv()
                copy(2 * x + core, mate, X + x).start()

    def settle(copy):
        copy(mate, mate, chip).wait_recv()

        @pl.loop(0, X)
        def _(x):
            @pl.when(x != chip)
            def _():
                copy(2 * x + 1 - core, mate, X + x).wait_recv()

    def finish(copy):
        copy(r, mate, chip).wait_send()

        @pl.loop(0, X)
        def _(x):
            @pl.when(x != chip)
            def _():
                copy(r, 2 * x + core, x).wait_send()
                copy(2 * x + core, mate, X + x).wait_send()

    spread_own(c_copy)

    crossed = pltpu.make_async_remote_copy(
        bdp, bdr, b_sem.at[0], b_sem.at[1], device_id={"row": z, "col": r}, device_id_type=MESH)

    @pl.when(r != z)
    def _():
        crossed.start()

    @pl.when(r == z)
    def _():
        bdr[...] = bdp[...]

    loads[4].wait()
    loads[5].wait()
    lj = liiv[0] + liiv[1]
    x1 = first_step(lj)
    x1h, x1l = split(x1)
    ljh, ljl = split(lj)
    lw = dot3(ljh, ljl, x1h, x1l)
    x2 = dot3(x1h, x1l, *split(lw)) - 2.0 * x1
    x2h, x2l = split(x2)
    nl = lj.shape[0]
    tl = lie.shape[2]
    TL = up128(tl)
    for b in range(2):
        lch[:, b * TL:b * TL + tl], lcl[:, b * TL:b * TL + tl] = split(liev[b])
        got = dot3(x2h, x2l, lch[:, b * TL:b * TL + tl], lcl[:, b * TL:b * TL + tl])
        lsv[b] = got
        lsh[:, b * TL:b * TL + tl], lsl[:, b * TL:b * TL + tl] = split(got)
    ls_out = pltpu.make_async_copy(lsv, lsolve, out_sem.at[0])
    ls_out.start()

    @pl.loop(0, C)
    def _(b):
        @pl.when(b != z)
        def _():
            jz_in(b).wait_recv()

    spread_own(j_copy)

    loads[6].wait()
    loads[7].wait()
    for a in range(2):
        let[...] = leiv[a].T

        @pl.loop(0, tl // nl)
        def _(m):
            rows = pl.ds(pl.multiple_of(m * nl, nl), nl)
            eh, el = split(let[rows])
            for b in range(2):
                cols = slice(b * TL, b * TL + tl)
                got = dot3(eh, el, lsh[:, cols], lsl[:, cols])
                lpv[a, b, rows] = got + leev[a, rows] if a == b else got
                pltpu.make_async_copy(lpv.at[a, b, rows], lparent.at[a, b, rows], lp_sem.at[2 * a + b, m]).start()

    mh = M // 2
    forward(1, 0, mh)
    relay(c_copy)
    settle(c_copy)
    for b in range(2):
        @pl.loop(0, R)
        def _(k):
            rows = pl.ds(pl.multiple_of(k * h, h), h)
            ch[rows, b * T:b * T + t], cl[rows, b * T:b * T + t] = split(cg[rows, b * t:(b + 1) * t])
    forward(1, mh, M)
    relay(j_copy)
    settle(j_copy)
    for a in range(R):
        for b in range(C):
            big[a * h:a * h + half, b * w:(b + 1) * w] = jg[a, b, :, :w]
            big[a * h + half:(a + 1) * h, b * w:(b + 1) * w] = jg[a, b, :, w:]
    joint = big[...]
    jh[...], jl[...] = split(joint)
    x1 = first_step(joint)
    big[...] = x1
    xh[...], xl[...] = split(x1)

    @pl.loop(0, R)
    def _(k):
        rows = pl.ds(pl.multiple_of(k * h, h), h)
        wh[rows], wl[rows] = split(dot3(jh[rows], jl[rows], xh[...], xl[...]))

    for s in range(2, C - 1):
        forward(s, 0, mh)

    @pl.loop(0, R)
    def _(k):
        rows = pl.ds(pl.multiple_of(k * h, h), h)
        jh[rows], jl[rows] = split(dot3(xh[rows], xl[rows], wh[...], wl[...]) - 2.0 * big[rows])

    for s in range(2, C - 1):
        forward(s, mh, M)

    @pl.loop(0, R)
    def _(k):
        rows = pl.ds(pl.multiple_of(k * h, h), h)
        for b in range(2):
            cols = slice(b * T, b * T + t)
            got = dot3(jh[rows], jl[rows], ch[:, cols], cl[:, cols])
            sh[rows, cols], sl[rows, cols] = split(got)

            @pl.when(k == r)
            def _():
                sv[b] = got

    s_out = pltpu.make_async_copy(sv, solve, out_sem.at[1])
    s_out.start()

    @pl.when(r != z)
    def _():
        crossed.wait_recv()

    fh, fl = split(bdr[...])
    for k in range(R):
        rows = slice(k * h, (k + 1) * h)
        got = dot3t(fh[0], fl[0], sh[rows, :t], sl[rows, :t])
        ivs[k] = got + dot3t(fh[1], fl[1], sh[rows, T:T + t], sl[rows, T:T + t])

    def iv_copy(k):
        return pltpu.make_async_remote_copy(
            ivs.at[k], ivr.at[z], iv_send.at[k], iv_recv.at[z], device_id={"row": k, "col": r}, device_id_type=MESH)

    def iv_in(c):
        return pltpu.make_async_remote_copy(
            ivs.at[r], ivr.at[c], iv_send.at[c], iv_recv.at[c], device_id={"row": z, "col": c}, device_id_type=MESH)

    for k in range(R):
        own = jnp.logical_and(r == k, r == z)

        @pl.when(jnp.logical_not(own))
        def _():
            iv_copy(k).start()

        @pl.when(own)
        def _():
            ivr[z] = ivs[k]

    loads[8].wait()

    @pl.loop(0, M)
    def _(m):
        @pl.when(z == C - 1)
        def _():
            @pl.loop(0, C - 1)
            def _(i):
                s = C - 2 - i
                e_copy(s, m, False).wait_recv()

        @pl.when(z == 0)
        def _():
            @pl.loop(1, C)
            def _(s):
                e_copy(s, m, True).wait_recv()

        rows = pl.ds(pl.multiple_of(m * tm, 8), tm)
        for c in range(C):
            for a in range(2):
                o = slice(a * tm, (a + 1) * tm)
                ah[o, c * u:(c + 1) * u], al[o, c * u:(c + 1) * u] = split(eg[c, rows, a * u:(a + 1) * u])
        for b in range(2):
            cols = slice(b * T, b * T + t)
            got = dot3(ah[...], al[...], sh[:, cols], sl[:, cols])
            for a in range(2):
                one = got[a * tm:(a + 1) * tm]
                pv[a, b, rows] = one + eev[a, rows] if a == b else one
                pltpu.make_async_copy(pv.at[a, b, rows], parent.at[a, b, rows], pm_sem.at[2 * a + b, m]).start()

    @pl.loop(0, C)
    def _(c):
        @pl.when(jnp.logical_not(jnp.logical_and(r == z, c == z)))
        def _():
            iv_in(c).wait_recv()

    total = ivr[0]
    for c in range(1, C):
        total = total + ivr[c]
    ivv[...] = total
    iv_out = pltpu.make_async_copy(ivv, iv, out_sem.at[2])
    iv_out.start()

    @pl.loop(0, C)
    def _(b):
        @pl.when(b != z)
        def _():
            jz(b).wait_send()

    finish(c_copy)
    finish(j_copy)

    @pl.when(r != z)
    def _():
        crossed.wait_send()

    for k in range(R):
        @pl.when(jnp.logical_not(jnp.logical_and(r == k, r == z)))
        def _():
            iv_copy(k).wait_send()

    @pl.loop(0, M)
    def _(m):
        @pl.when(can_up)
        def _():
            @pl.loop(0, z + 1)
            def _(s):
                e_copy(s, m, True).wait_send()

        @pl.when(can_dn)
        def _():
            @pl.loop(z, C)
            def _(s):
                e_copy(s, m, False).wait_send()

        rows = pl.ds(pl.multiple_of(m * tm, 8), tm)
        for a in range(2):
            for b in range(2):
                pltpu.make_async_copy(pv.at[a, b, rows], parent.at[a, b, rows], pm_sem.at[2 * a + b, m]).wait()

    @pl.loop(0, tl // nl)
    def _(m):
        rows = pl.ds(pl.multiple_of(m * nl, nl), nl)
        for a in range(2):
            for b in range(2):
                pltpu.make_async_copy(lpv.at[a, b, rows], lparent.at[a, b, rows], lp_sem.at[2 * a + b, m]).wait()

    ls_out.wait()
    s_out.wait()
    iv_out.wait()


def fused(R, C, ee, ei, ie, ii, bd, lee, lei, lie, lii):
    lee, lei, lie, lii = lee[0], jnp.swapaxes(lei[0], 1, 2), lie[0], lii[0]
    ei, bd = jnp.swapaxes(ei, 1, 2), jnp.swapaxes(bd, 1, 2)
    h, w = ii.shape[1:]
    u, t = ei.shape[1:]
    nl, tl = lie.shape[1:]
    T, TL = up128(t), up128(tl)
    n = R * h
    q = bd.shape[1]
    M = 6
    tm = t // M
    V = pltpu.VMEM
    D = pltpu.SemaphoreType.DMA
    scratch = [
        V((C, t, 2 * u), F32), V((n, 2 * t), F32), V((R, C, h // 2, 2 * w), F32),
        V((2, q, t), F32), V((2, q, t), F32), V((R, q, h), F32), V((C, q, h), F32),
        V(ei.shape, F32), V(ie.shape, F32), V(ii.shape, F32), V(ee.shape, F32),
        V(lee.shape, F32), V(lei.shape, F32), V((tl, nl), F32), V(lie.shape, F32), V(lii.shape, F32),
        V((2, 2, t, t), F32), V((2, h, t), F32), V((q, h), F32), V((2, 2, tl, tl), F32), V((2, nl, tl), F32),
        V((n, n), F32), V((n, n), BF), V((n, n), BF), V((n, n), BF), V((n, n), BF), V((n, n), BF), V((n, n), BF),
        V((n, 2 * T), BF), V((n, 2 * T), BF), V((n, 2 * T), BF), V((n, 2 * T), BF),
        V((nl, 2 * TL), BF), V((nl, 2 * TL), BF), V((nl, 2 * TL), BF), V((nl, 2 * TL), BF),
        V((2 * tm, n), BF), V((2 * tm, n), BF),
        D((9,)), D((C, M)), D((C, M)), D((C, M)), D((C,)), D((C,)), D((R,)), D((R,)), D((R,)), D((R,)),
        D((2,)), D((R,)), D((C,)), D((3,)), D((4, tl // nl)), D((4, M)),
    ]
    outs = (
        jax.ShapeDtypeStruct((2, 2, t, t), F32),
        jax.ShapeDtypeStruct((2, h, t), F32),
        jax.ShapeDtypeStruct((q, h), F32),
        jax.ShapeDtypeStruct((2, 2, tl, tl), F32),
        jax.ShapeDtypeStruct((2, nl, tl), F32),
    )
    got = pl.pallas_call(
        functools.partial(kernel, R, C, M),
        out_shape=outs,
        in_specs=[pl.BlockSpec(memory_space=pl.ANY)] * 9,
        out_specs=[pl.BlockSpec(memory_space=pl.ANY)] * 5,
        scratch_shapes=scratch,
        compiler_params=pltpu.CompilerParams(
            collective_id=0, has_side_effects=True, vmem_limit_bytes=60 * 1024 * 1024),
        cost_estimate=pl.CostEstimate(flops=18 * n * n * t * 4, bytes_accessed=24 * t * t * 4, transcendentals=0),
    )(ee, ei, ie, ii, bd, lee, lei, lie, lii)
    return got[0], got[1], got[2].T, got[3][None], got[4][None]


def fits(R, C, shapes):
    h, w = shapes[3][1] // R, shapes[3][2] // C
    t, u = shapes[1][1] // R, shapes[1][2] // C
    q = shapes[4][2] // C
    nl, tl = shapes[7][2:]
    boxes = shapes[5][0]
    return (
        R == C and R % 2 == 0 and C >= 3 and h == w == u and h % 16 == 0 and (2 * u) % 128 == 0 and t % 48 == 0
        and q % 16 == 0 and tl % nl == 0 and nl % 16 == 0
    )


def matmul(a, b):
    return jnp.dot(a, b, precision=lax.Precision.HIGHEST, preferred_element_type=jnp.float32)


def panel(block):
    return lax.all_gather(block, "col", axis=1, tiled=True)


def fold_product(left_rows, right_block):
    return matmul(left_rows, lax.all_gather(right_block, "row", axis=0, tiled=True))


def product(left_block, right_block):
    return fold_product(panel(left_block), right_block)


def merge_local(ee, ei, ie, ii):
    side = ii.shape[1]
    third = ee.shape[1]
    joint = ii[0] + ii[1]
    eye = jnp.eye(side, dtype=jnp.float32)
    current = eye / jnp.diagonal(joint)[None, :]
    for step in range(ITERS):
        current = 2.0 * current - matmul(current, matmul(joint, current))
    coupling = jnp.concatenate([ie[0], ie[1]], axis=1)
    solution = -matmul(current, coupling)
    solve = jnp.stack([solution[:, :third], solution[:, third:]])
    lifted = matmul(ei.reshape(2 * third, side), solution)
    lifted = lifted.reshape(2, third, 2, third).transpose(0, 2, 1, 3)
    pairs = jnp.eye(2, dtype=jnp.float32)
    parent = lifted + pairs[:, :, None, None] * ee[:, None]
    return (parent, solve)


def shards(
    ext_ext,
    ext_int,
    int_ext,
    int_int,
    boundary_data,
    leaf_ext_ext,
    leaf_ext_int,
    leaf_int_ext,
    leaf_int_int,
):
    n_col = lax.axis_size("col")
    joint = int_int[0] + int_int[1]
    rows_here = joint.shape[0]
    cols_here = joint.shape[1]
    third = ext_ext.shape[2]
    coupling = jnp.concatenate([int_ext[0], int_ext[1]], axis=1)
    global_row = lax.axis_index("row") * rows_here + lax.broadcasted_iota(jnp.int32, joint.shape, 0)
    global_col = lax.axis_index("col") * cols_here + lax.broadcasted_iota(jnp.int32, joint.shape, 1)
    on_diag = global_row == global_col
    current = jnp.where(on_diag, 1.0 / jnp.where(on_diag, joint, 1.0), 0.0)
    for step in range(ITERS):
        current = 2.0 * current - product(current, product(joint, current))
    solution = -product(current, coupling)
    leaf_parent, leaf_solve = jax.vmap(merge_local)(
        leaf_ext_ext, leaf_ext_int, leaf_int_ext, leaf_int_int
    )
    solve_op = jnp.stack([solution[:, :third], solution[:, third:]])
    ext_rows = ext_int.shape[1]
    lifted = product(ext_int.reshape(2 * ext_rows, ext_int.shape[2]), solution)
    lifted = lifted.reshape(2, ext_rows, 2, third).transpose(0, 2, 1, 3)
    pairs = jnp.eye(2, dtype=jnp.float32)
    parent_map = lifted + pairs[:, :, None, None] * ext_ext[:, None]
    operator_rows = panel(solution)
    operator_rows = operator_rows.reshape(rows_here, n_col, 2, third).transpose(0, 2, 1, 3)
    operator_rows = operator_rows.reshape(rows_here, 2, n_col * third)
    interface_values = jnp.einsum(
        "pcn,cnq->pq",
        operator_rows,
        lax.all_gather(boundary_data, "row", axis=1, tiled=True),
        precision=lax.Precision.HIGHEST,
    )
    return (parent_map, solve_op, interface_values, leaf_parent, leaf_solve)


def solution(mesh):
    in_specs = (
        P("dom", "row", "col"),
        P("dom", "row", "col"),
        P("dom", "row", "col"),
        P("dom", "row", "col"),
        P("dom", "row", "col"),
        P(("dom", "row", "col"), None, None, None),
        P(("dom", "row", "col"), None, None, None),
        P(("dom", "row", "col"), None, None, None),
        P(("dom", "row", "col"), None, None, None),
    )
    out_specs = (
        P("dom", None, "row", "col"),
        P("dom", "row", "col"),
        P(("dom", "row"), "col"),
        P(("dom", "row", "col"), None, None, None, None),
        P(("dom", "row", "col"), None, None, None),
    )

    def run(*args):
        shapes = [a.shape for a in args]
        R, C = mesh.shape["row"], mesh.shape["col"]
        one_box = shapes[5][0] == mesh.shape["dom"] * R * C
        two_maps = shapes[0][0] == 2 * mesh.shape["dom"]
        body = functools.partial(fused, R, C) if one_box and two_maps and fits(R, C, shapes) else shards
        return jax.shard_map(body, mesh=mesh, in_specs=in_specs, out_specs=out_specs, check_vma=False)(*args)

    return run
```
